256 devices in a mesh: dp: 16 (over z_hi, y), row: 2 (over z_lo), col: 8 (over x, core).
Axes of the slice: x: 4, y: 4, z: 8 (z_hi: 4, z_lo: 2; z = z_hi * 2 + z_lo), core: 2. Of those that a mesh axis runs over, the one named last changes fastest.
Arguments:
- activations: bfloat16 [16384, 4096], P('dp', 'row'), may hold values from -160 to 160, as said below
- cotangent: bfloat16 [16384, 16384], P('dp', 'col'), may hold values from -0.03125 to 0.03125, as said below
- row_old: float32 [4096], P(('row', 'dp')), may hold values from 1 to 70, as said below
- col_old: float32 [16384], P('col'), may hold values from 0.02 to 0.3
Outputs:
- update: float32 [4096, 16384], P(('row', 'dp'), 'col')
- row_new: float32 [4096], P(('row', 'dp'))
- col_new: float32 [16384], P('col')
- update_rms: float32 [], replicated
The draws below stay inside these ranges and needn't reach their ends.
Inputs may be any that keep to these rules, and one draw needn't show every extreme that they name: activations of feature columns of differing scales. cotangent columns of differing scales. `row_old`: positive entries of differing scales.
All inputs are finite; a program needn't handle non-finite values.
Results may differ from the reference program's by a relative error of at most 0.0003.
Values sent between devices are 32-bit elements; how exact they have to be, the bound alone decides.
No kernel may reach another device: no remote copies, remote signals or barrier semaphores. Data moves between devices by JAX's collectives and lax.ppermute only.
A program may use at most 128 MiB of HBM per device.

```python
import math
import jax
import jax.numpy as jnp
from jax import lax

D = 4096
FF = 16384
TOK_DEV = 1024
TOKENS = 16384
N_DP = 16
N_ROW = 2


def column_scales(key, count):
    spread = jnp.exp(jax.random.uniform(key, (count,), jnp.float32) * math.log(3.2))
    ramp = 1.0 + 2.0 * jnp.arange(count, dtype=jnp.float32) / count
    return spread * ramp


def owner_ramp(count):
    positions = jnp.arange(count, dtype=jnp.int32)
    block = count // (N_ROW * N_DP)
    owner = positions // block % N_DP
    frac = owner.astype(jnp.float32) / (N_DP - 1)
    return jnp.exp(frac * math.log(10.0))


def base_values(key, shape):
    return jax.random.truncated_normal(key, -4.0, 4.0, shape, jnp.float32)


def draw_activations(key, part):
    key = jax.random.fold_in(key, 11)
    first, second = jax.random.split(key)
    spread = jnp.exp(jax.random.uniform(second, (D,), jnp.float32) * math.log(2.0))
    values = base_values(first, (TOKENS, D)) * (spread * owner_ramp(D))[None, :]
    return values.astype(jnp.bfloat16)


def draw_cotangent(key, part):
    key = jax.random.fold_in(key, 23)
    first, second = jax.random.split(key)
    factor = 0.1 * TOKENS ** (-0.5)
    values = base_values(first, (TOKENS, FF)) * column_scales(second, FF)[None, :] * factor
    return values.astype(jnp.bfloat16)


def draw_row_old(key, part):
    key = jax.random.fold_in(key, 37)
    spread = jnp.exp(jax.random.uniform(key, (D,), jnp.float32) * math.log(2.0))
    return 1.7 * spread * owner_ramp(D)


def levels(stream_key, shape, shards, least, high):
    level, own = 1.0, jax.random.fold_in(stream_key, 6)
    for position, blocks in shards:
        heights = jnp.exp(jax.random.uniform(jax.random.fold_in(own, position), (blocks,), jnp.float32, least / len(shards), high / len(shards)))
        level = level * jnp.repeat(heights, shape[position] // blocks).reshape([-1 if axis == position else 1 for axis in range(len(shape))])
    return level


def setup_inputs(seed: int = 0) -> dict:
    arg_keys = jax.random.split(jax.random.key(seed), 5)
    activations = draw_activations(jax.random.fold_in(arg_keys[4], 71), 0)
    cotangent = draw_cotangent(jax.random.fold_in(arg_keys[4], 71), 0)
    row_old = draw_row_old(jax.random.fold_in(arg_keys[4], 71), 0)
    col_old = jnp.clip(jnp.exp(math.log(0.3) - 2.7080503 * jax.random.uniform(arg_keys[3], (FF,), jnp.float32) ** levels(arg_keys[3], (FF,), ((0, 8),), -0.2, 0.2)), 0.02, 0.3)
    return {"activations": activations, "cotangent": cotangent, "row_old": row_old, "col_old": col_old}


DECAY = 0.5
EPS_ONE = 1e-30
CLIP = 0.25

def reference(activations, cotangent, row_old, col_old):
    x_blocks = activations.reshape(N_DP, TOK_DEV, D)
    g_blocks = cotangent.reshape(N_DP, TOK_DEV, FF)

    def add_block(total, pair):
        x_blk, g_blk = pair
        partial_value = jnp.dot(x_blk.T, g_blk, preferred_element_type=jnp.float32)
        return (total + partial_value, None)
    grad, _ = lax.scan(add_block, jnp.zeros((D, FF), jnp.float32), (x_blocks, g_blocks))
    squares = grad * grad + EPS_ONE
    row_new = DECAY * row_old + (1.0 - DECAY) * lax.optimization_barrier(jnp.mean(squares, axis=1))
    col_new = DECAY * col_old + (1.0 - DECAY) * lax.optimization_barrier(jnp.mean(squares, axis=0))
    row_mean = jnp.mean(row_new)
    raw = grad / jnp.sqrt(row_new[:, None] * col_new[None, :] / row_mean)
    update_rms = jnp.sqrt(jnp.mean(raw * raw))
    update = raw / jnp.maximum(1.0, update_rms / CLIP)
    return (update, row_new, col_new, update_rms)
```

```python
import jax
import jax.numpy as jnp
from jax import lax
from jax.sharding import Mesh, PartitionSpec as P

D = 4096
FF = 16384


DECAY = 0.5
EPS_ONE = 1e-30
CLIP = 0.25

AXES = ("zh", "y", "zl", "x", "c")
CHUNKS = (
    ("zh", 0, 256),
    ("zh", 256, 384),
    ("y", 384, 896),
    ("y", 896, 1408),
    ("y", 1408, 1792),
    ("y", 1792, 2048),
)
ORDER = {
    "y": ((2, 3), (0, 1), (4, 5)),
    "zh": ((0, 1), (2, 3), (4, 5)),
}
DEPTH = 2


def ring_step(value, axis):
    pairs = []
    for i in range(4):
        pairs.append((2 * i, 2 * ((i + 1) % 4)))
        pairs.append((2 * i + 1, 2 * ((i + 3) % 4) + 1))
    return lax.ppermute(value, (axis, "c"), pairs)


def spread_sum(value, axes, count):
    copies = jnp.broadcast_to(value[None], (count,) + value.shape)
    return jnp.sum(lax.all_to_all(copies, axes, 0, 0), axis=0)


def summed_product(activations, cotangent):
    way = 1 - 2 * lax.axis_index("c")
    place = {axis: lax.axis_index(axis) for axis in ("zh", "y")}
    blocks = activations.reshape(-1, 4, 4, 128)
    lhs = {}

    def owner(axis, step):
        return (place[axis] + 4 - way * (step + 1)) % 4

    def product(chunk, step):
        axis, start, stop = CHUNKS[chunk]
        if (axis, step) not in lhs:
            rows = lax.dynamic_index_in_dim(
                blocks, owner(axis, step), 1 if axis == "zh" else 2, keepdims=False)
            lhs[axis, step] = rows.reshape(-1, 512)
        return lax.dot_general(
            lhs[axis, step], cotangent[:, start:stop], (((0,), (0,)), ((), ())),
            preferred_element_type=jnp.float32)

    queues = {axis: [] for axis in ("zh", "y")}
    for axis, groups in ORDER.items():
        for group in groups:
            for step in range(3):
                queues[axis] += [(chunk, step) for chunk in group]
    sent = {axis: [] for axis in queues}
    held, first_sum, grads = {}, {}, {}

    def ready(axis, chunk):
        return CHUNKS[chunk][0] == axis or chunk in first_sum

    def block(axis, chunk, step):
        if CHUNKS[chunk][0] == axis:
            return product(chunk, step)
        return lax.dynamic_index_in_dim(first_sum[chunk], owner(axis, step), 0, keepdims=False)

    def advance(axis):
        chunk, step = queues[axis].pop(0)
        value = block(axis, chunk, step)
        if step:
            value = value + held[axis, chunk]
        if len(sent[axis]) >= DEPTH:
            value, _ = lax.optimization_barrier((value, sent[axis][-DEPTH]))
        moved = ring_step(value, axis)
        sent[axis].append(moved)
        held[axis, chunk] = moved
        if step == 2:
            total = moved + block(axis, chunk, 3)
            if CHUNKS[chunk][0] == axis:
                first_sum[chunk] = total.reshape(4, 128, -1)
            else:
                grads[chunk] = total

    while any(queues.values()):
        for axis in queues:
            if queues[axis] and ready(axis, queues[axis][0][0]):
                advance(axis)
    return jnp.concatenate([grads[i] for i in range(len(CHUNKS))], axis=1)


def per_device(activations, cotangent, row_old, col_old):
    grad = summed_product(activations, cotangent)
    square = grad * grad
    squares = square + EPS_ONE
    row_total = spread_sum(jnp.sum(squares, axis=1), ("x", "c"), 8)
    row_new = DECAY * row_old + (1.0 - DECAY) * (row_total / FF)
    local = jnp.concatenate([
        jnp.sum(squares, axis=0),
        jnp.sum(square / row_new[:, None], axis=0),
        row_new,
    ])
    local = spread_sum(local, ("zh", "y", "zl"), 32)
    cols = col_old.shape[0]
    col_new = DECAY * col_old + (1.0 - DECAY) * (local[:cols] / D)
    row_mean = jnp.sum(local[2 * cols:]) / D
    share = jnp.sum(local[cols:2 * cols] / col_new) * row_mean
    total_sq = spread_sum(jnp.broadcast_to(share, (128,)), ("x", "c"), 8)[0]
    update_rms = jnp.sqrt(total_sq / (D * FF))
    scale = jnp.sqrt(row_mean) / jnp.maximum(1.0, update_rms / CLIP)
    update = grad * (scale / jnp.sqrt(row_new))[:, None] * (1.0 / jnp.sqrt(col_new))[None, :]
    return (update, row_new, col_new, update_rms)


def solution(mesh):
    mesh = Mesh(mesh.devices.reshape(4, 4, 2, 4, 2), AXES)
    dp, col = ("zh", "y"), ("x", "c")
    in_specs = (P(dp, "zl"), P(dp, col), P(("zl",) + dp), P(col))
    out_specs = (P(("zl",) + dp, col), P(("zl",) + dp), P(col), P())
    return jax.shard_map(
        per_device, mesh=mesh, in_specs=in_specs, out_specs=out_specs, check_vma=False
    )
```

```python
import jax
import jax.numpy as jnp
from jax import lax
from jax.experimental import pallas as pl
from jax.experimental.pallas import tpu as pltpu
from jax.sharding import Mesh, PartitionSpec as P

D = 4096
FF = 16384


DECAY = 0.5
EPS_ONE = 1e-30
CLIP = 0.25

AXES = ("zh", "y", "zl", "x", "c")
COLS = ((0, 512), (512, 1024), (1024, 1408), (1408, 1664), (1664, 2048))


def ring_step(value, axis):
    pairs = []
    for i in range(4):
        pairs.append((2 * i, 2 * ((i + 1) % 4)))
        pairs.append((2 * i + 1, 2 * ((i + 3) % 4) + 1))
    return lax.ppermute(value, (axis, "c"), pairs)


def spread_sum(value, axes, count):
    copies = jnp.broadcast_to(value[None], (count,) + value.shape)
    return jnp.sum(lax.all_to_all(copies, axes, 0, 0), axis=0)


def after(value, other):
    return lax.optimization_barrier((value, other))[0]


def product_kernel(blocks, rows, cols, out):
    out[...] = lax.dot_general(
        rows[...], cols[...], (((0,), (0,)), ((), ())), preferred_element_type=jnp.float32)


def block_product(blocks, rows, cols):
    depth, width = cols.shape
    return pl.pallas_call(
        product_kernel,
        grid_spec=pltpu.PrefetchScalarGridSpec(
            num_scalar_prefetch=1,
            grid=(4,),
            in_specs=[
                pl.BlockSpec((depth, 128), lambda i, blocks: (0, blocks[i])),
                pl.BlockSpec((depth, width), lambda i, blocks: (0, 0)),
            ],
            out_specs=pl.BlockSpec((128, width), lambda i, blocks: (i, 0)),
        ),
        out_shape=jax.ShapeDtypeStruct((512, width), jnp.float32),
        compiler_params=pltpu.CompilerParams(vmem_limit_bytes=8 * 2**20),
        cost_estimate=pl.CostEstimate(
            flops=2 * 512 * depth * width, bytes_accessed=4 * 2**20, transcendentals=0),
    )(blocks, rows, cols)


class Order:
    def __init__(self):
        self.last = None

    def __call__(self, value):
        if self.last is not None:
            value = after(value, self.last)
        self.last = value
        return value


class Chain:
    def __init__(self, order, axis, add):
        self.order, self.axis, self.add = order, axis, add
        self.step, self.value = 0, add(0, None)

    def start(self):
        self.moved = ring_step(self.order(self.value), self.axis)

    def done(self):
        self.step += 1
        self.value = self.add(self.step, self.order(self.moved))

    def turn(self):
        self.done()
        self.start()


def summed_product(activations, cotangent):
    way = 1 - 2 * lax.axis_index("c")
    place = {axis: lax.axis_index(axis) for axis in ("zh", "y")}
    index = jnp.arange(4, dtype=jnp.int32)
    order = Order()
    lhs = {}

    def owner(axis, step):
        return (place[axis] + 4 - way * (step + 1)) % 4

    def rows(source, axis, step):
        source = source.reshape(-1, 4, 4, 128)
        found = lax.dynamic_index_in_dim(
            source, owner(axis, step), 1 if axis == "zh" else 2, keepdims=False)
        return found.reshape(-1, 512)

    def first_product(axis, chunk):
        mine = owner(axis, 0).astype(jnp.int32)
        blocks = 4 * index + mine if axis == "y" else 4 * mine + index
        return block_product(blocks, activations, cotangent[:, slice(*COLS[chunk])])

    def product_chain(axis, chunk, early=False):
        def add(step, moved):
            if early and step == 0:
                return first_product(axis, chunk)
            value = lax.dot_general(
                lhs[axis, step], cotangent[:, slice(*COLS[chunk])], (((0,), (0,)), ((), ())),
                preferred_element_type=jnp.float32)
            return value if moved is None else moved + value

        return Chain(order, axis, add)

    def next_chain(chain):
        axis = "zh" if chain.axis == "y" else "y"
        total = chain.value.reshape(4, 128, -1)

        def add(step, moved):
            mine = lax.dynamic_index_in_dim(total, owner(axis, step), 0, keepdims=False)
            return mine if moved is None else moved + mine

        return Chain(order, axis, add)

    a = product_chain("y", 0, True)
    a.start()
    b = product_chain("y", 1, True)
    b.start()
    e = product_chain("zh", 4, True)
    e.start()
    rest = order(activations)
    lhs.update({(axis, step): rows(rest, axis, step) for axis in place for step in range(4)})
    for step in range(2):
        a.turn()
        b.turn()
        e.turn()
    c, d = product_chain("y", 2), product_chain("y", 3)
    a.done()
    c.start()
    a = next_chain(a)
    a.start()
    b.done()
    d.start()
    e.done()
    b = next_chain(b)
    b.start()
    e = next_chain(e)
    e.start()
    for step in range(2):
        c.turn()
        a.turn()
        e.turn()
        d.turn()
        b.turn()
    c.done()
    c = next_chain(c)
    c.start()
    a.done()
    e.done()
    d.done()
    d = next_chain(d)
    d.start()
    b.done()
    for step in range(2):
        c.turn()
        d.turn()
    c.done()
    d.done()
    return [chain.value for chain in (a, b, c, d, e)]


def per_device(activations, cotangent, row_old, col_old):
    grads = summed_product(activations, cotangent)
    squares = [g * g + EPS_ONE for g in grads]
    col_total = jnp.concatenate([jnp.sum(s, axis=0) for s in squares])
    col_total = spread_sum(col_total, ("zh", "y", "zl"), 32)
    row_total = sum(jnp.sum(s, axis=1) for s in squares)
    row_total = row_total + lax.ppermute(row_total, "c", [(0, 1), (1, 0)])
    row_total = row_total + sum(
        lax.ppermute(row_total, "x", [(i, (i + d) % 4) for i in range(4)]) for d in (1, 2, 3))
    row_new = DECAY * row_old + (1.0 - DECAY) * (row_total / FF)
    col_new = DECAY * col_old + (1.0 - DECAY) * (col_total / D)
    grad = jnp.concatenate(grads, axis=1)
    share = jnp.sum((grad * grad / row_new[:, None]) / col_new[None, :])
    pair = jnp.stack([share, jnp.sum(row_new)])
    pair = spread_sum(pair, AXES, 256)
    row_mean = pair[1] / (8 * D)
    update_rms = jnp.sqrt(pair[0] * row_mean / (D * FF))
    scale = jnp.sqrt(row_mean) / jnp.maximum(1.0, update_rms / CLIP)
    update = grad * (scale / jnp.sqrt(row_new))[:, None] * (1.0 / jnp.sqrt(col_new))[None, :]
    return (update, row_new, col_new, update_rms)


def solution(mesh):
    mesh = Mesh(mesh.devices.reshape(4, 4, 2, 4, 2), AXES)
    dp, col = ("zh", "y"), ("x", "c")
    in_specs = (P(dp, "zl"), P(dp, col), P(("zl",) + dp), P(col))
    out_specs = (P(("zl",) + dp, col), P(("zl",) + dp), P(col), P())
    return jax.shard_map(
        per_device, mesh=mesh, in_specs=in_specs, out_specs=out_specs, check_vma=False
    )
```

```python
import jax
import jax.numpy as jnp
from jax import lax
from jax.experimental import pallas as pl
from jax.experimental.pallas import tpu as pltpu
from jax.sharding import Mesh, PartitionSpec as P

D = 4096
FF = 16384


DECAY = 0.5
EPS_ONE = 1e-30
CLIP = 0.25

AXES = ("zh", "y", "zl", "x", "c")
COLS = {
    "a": (0, 256), "b": (256, 768), "c": (768, 1280),
    "d": (1280, 1536), "f": (1536, 1664), "e": (1664, 2048),
}


def swap(value, axis, step):
    pairs = []
    for i in range(4):
        for core in range(2):
            other = i ^ 1 if core == step else i ^ 3
            pairs.append((2 * i + core, 2 * other + core))
    return lax.ppermute(value, (axis, "c"), pairs)


def spread_sum(value, axes, count):
    copies = jnp.broadcast_to(value[None], (count,) + value.shape)
    return jnp.sum(lax.all_to_all(copies, axes, 0, 0), axis=0)


def after(value, other):
    return lax.optimization_barrier((value, other))[0]


def first_kernel(blocks, rows, cols, out):
    out[...] = lax.dot_general(
        rows[...], cols[...], (((0,), (0,)), ((), ())), preferred_element_type=jnp.float32)


def second_kernel(blocks, rows, cols, out, by_y, by_zh):
    part = rows[...].T
    by_y[...] = part
    by_zh[...] = part

    @pl.when(pl.program_id(0) < 8)
    def _():
        out[...] = jnp.dot(part, cols[...], preferred_element_type=jnp.float32)


def early_product(kernel, blocks, rows, cols):
    depth, width = cols.shape
    count = blocks.shape[0]
    out_specs = [pl.BlockSpec((128, width), lambda i, blocks: (jnp.minimum(i, 7), 0))]
    out_shape = [jax.ShapeDtypeStruct((1024, width), jnp.float32)]
    if count == 16:
        out_specs += [
            pl.BlockSpec((128, depth), lambda i, blocks: (i, 0)),
            pl.BlockSpec((128, depth), lambda i, blocks: (4 * (i % 4) + i // 4, 0)),
        ]
        out_shape += [jax.ShapeDtypeStruct((2048, depth), rows.dtype)] * 2
    return pl.pallas_call(
        kernel,
        grid_spec=pltpu.PrefetchScalarGridSpec(
            num_scalar_prefetch=1,
            grid=(count,),
            in_specs=[
                pl.BlockSpec((depth, 128), lambda i, blocks: (0, blocks[i])),
                pl.BlockSpec((depth, width), lambda i, blocks: (0, 0)),
            ],
            out_specs=out_specs,
        ),
        out_shape=out_shape,
        compiler_params=pltpu.CompilerParams(vmem_limit_bytes=8 * 2**20),
        cost_estimate=pl.CostEstimate(
            flops=2 * 1024 * depth * width, bytes_accessed=8 * 2**20, transcendentals=0),
    )(blocks, rows, cols)


class Order:
    def __init__(self):
        self.last = None

    def __call__(self, value):
        if self.last is not None:
            value = after(value, self.last)
        self.last = value
        return value


class Chain:
    def __init__(self, order, axis, part):
        self.order, self.axis, self.part = order, axis, part

    def start(self):
        self.moved = swap(self.order(self.part(0)), self.axis, 0)

    def turn(self):
        got = self.order(self.moved)
        half = got.shape[0] // 2
        self.kept = got[:half]
        self.moved = swap(self.order(got[half:] + self.part(1)), self.axis, 1)

    def done(self):
        self.value = (self.order(self.moved) + self.kept) + self.part(2)


def summed_product(activations, cotangent):
    core = lax.axis_index("c")
    order = Order()

    def owners(axis):
        mine = lax.axis_index(axis)
        near, far = mine ^ 1, mine ^ 3
        return jnp.stack([
            jnp.where(core == 0, near, far), mine ^ 2, jnp.where(core == 0, far, near), mine,
        ]).astype(jnp.int32)

    def columns(chunk):
        return cotangent[:, slice(*COLS[chunk])]

    def quarters(rows):
        size = rows.shape[0] // 4
        return (rows[:2 * size], rows[2 * size:3 * size], rows[3 * size:])

    def product_chain(axis, chunk, first=None):
        def part(i):
            if i == 0 and first is not None:
                return first
            return jnp.dot(lhs[axis][i], columns(chunk), preferred_element_type=jnp.float32)

        return Chain(order, axis, part)

    def next_chain(chain):
        parts = quarters(chain.value)
        return Chain(order, "zh" if chain.axis == "y" else "y", lambda i: parts[i])

    blocks = (owners("y")[:, None] + 4 * owners("zh")[None, :]).reshape(16)
    first, = early_product(first_kernel, blocks[:8], activations, columns("a"))
    a = product_chain("y", "a", first)
    a.start()
    first, by_y, by_zh = early_product(second_kernel, blocks, order(activations), columns("b"))
    lhs = {"y": quarters(by_y), "zh": quarters(by_zh)}
    b = product_chain("y", "b", first)
    b.start()
    c, d, f = (product_chain("y", chunk) for chunk in "cdf")
    e = product_chain("zh", "e")
    e.start()
    a.turn()
    a.done()
    c.start()
    a = next_chain(a)
    a.start()
    b.turn()
    e.turn()
    a.turn()
    b.done()
    c.turn()
    b = next_chain(b)
    b.start()
    a.done()
    e.done()
    e = next_chain(e)
    e.start()
    d.start()
    b.turn()
    c.done()
    c = next_chain(c)
    c.start()
    f.start()
    d.turn()
    e.turn()
    f.turn()
    b.done()
    c.turn()
    d.done()
    d = next_chain(d)
    d.start()
    f.done()
    f = next_chain(f)
    f.start()
    d.turn()
    f.turn()
    e.done()
    c.done()
    d.done()
    f.done()
    return [chain.value for chain in (a, b, c, d, f, e)]


def per_device(activations, cotangent, row_old, col_old):
    grads = summed_product(activations, cotangent)
    squares = [g * g + EPS_ONE for g in grads]
    col_total = jnp.concatenate([jnp.sum(s, axis=0) for s in squares])
    row_total = sum(jnp.sum(s, axis=1) for s in squares)
    col_total = spread_sum(col_total, ("zh", "y", "zl"), 32)
    col_new = DECAY * col_old + (1.0 - DECAY) * (col_total / D)
    grad = jnp.concatenate(grads, axis=1)
    rows = jnp.stack([row_total, jnp.sum(grad * grad / col_new[None, :], axis=1)])
    rows = rows + lax.ppermute(rows, "c", [(0, 1), (1, 0)])
    rows = rows + sum(
        lax.ppermute(rows, "x", [(i, (i + d) % 4) for i in range(4)]) for d in (1, 2, 3))
    row_new = DECAY * row_old + (1.0 - DECAY) * (rows[0] / FF)
    pair = jnp.concatenate([rows[1] / row_new, row_new])
    pair = spread_sum(pair, ("zh", "y", "zl"), 32)
    row_mean = jnp.sum(pair[128:]) / D
    pair = jnp.sum(pair[:128])[None]
    update_rms = jnp.sqrt(pair[0] * row_mean / (D * FF))
    scale = jnp.sqrt(row_mean) / jnp.maximum(1.0, update_rms / CLIP)
    update = grad * (scale / jnp.sqrt(row_new))[:, None] * (1.0 / jnp.sqrt(col_new))[None, :]
    return (update, row_new, col_new, update_rms)


def solution(mesh):
    mesh = Mesh(mesh.devices.reshape(4, 4, 2, 4, 2), AXES)
    dp, col = ("zh", "y"), ("x", "c")
    in_specs = (P(dp, "zl"), P(dp, col), P(("zl",) + dp), P(col))
    out_specs = (P(("zl",) + dp, col), P(("zl",) + dp), P(col), P())
    return jax.shard_map(
        per_device, mesh=mesh, in_specs=in_specs, out_specs=out_specs, check_vma=False
    )
```

```python
import jax
import jax.numpy as jnp
from jax import lax
from jax.experimental import pallas as pl
from jax.experimental.pallas import tpu as pltpu
from jax.sharding import Mesh, PartitionSpec as P

D = 4096
FF = 16384


DECAY = 0.5
EPS_ONE = 1e-30
CLIP = 0.25

AXES = ("zh", "y", "zl", "x", "c")
COLS = {
    "a": (0, 256), "b": (256, 768), "c": (768, 1280),
    "d": (1280, 1536), "f": (1536, 1664), "e": (1664, 2048),
}


def swap(value, axis, step):
    pairs = []
    for i in range(4):
        for core in range(2):
            other = i ^ 1 if core == step else i ^ 3
            pairs.append((2 * i + core, 2 * other + core))
    return lax.ppermute(value, (axis, "c"), pairs)


def spread_sum(value, axes, count):
    copies = jnp.broadcast_to(value[None], (count,) + value.shape)
    return jnp.sum(lax.all_to_all(copies, axes, 0, 0), axis=0)


def after(value, other):
    return lax.optimization_barrier((value, other))[0]


def first_kernel(blocks, rows, cols, out):
    out[...] = lax.dot_general(
        rows[...], cols[...], (((0,), (0,)), ((), ())), preferred_element_type=jnp.float32)


def second_kernel(blocks, rows, cols, out, by_y, by_zh):
    part = rows[...].T
    by_y[...] = part
    by_zh[...] = part

    @pl.when(pl.program_id(0) < 8)
    def _():
        out[...] = jnp.dot(part, cols[...], preferred_element_type=jnp.float32)


def early_product(kernel, blocks, rows, cols):
    depth, width = cols.shape
    count = blocks.shape[0]
    out_specs = [pl.BlockSpec((128, width), lambda i, blocks: (jnp.minimum(i, 7), 0))]
    out_shape = [jax.ShapeDtypeStruct((1024, width), jnp.float32)]
    if count == 16:
        out_specs += [
            pl.BlockSpec((128, depth), lambda i, blocks: (i, 0)),
            pl.BlockSpec((128, depth), lambda i, blocks: (4 * (i % 4) + i // 4, 0)),
        ]
        out_shape += [jax.ShapeDtypeStruct((2048, depth), rows.dtype)] * 2
    return pl.pallas_call(
        kernel,
        grid_spec=pltpu.PrefetchScalarGridSpec(
            num_scalar_prefetch=1,
            grid=(count,),
            in_specs=[
                pl.BlockSpec((depth, 128), lambda i, blocks: (0, blocks[i])),
                pl.BlockSpec((depth, width), lambda i, blocks: (0, 0)),
            ],
            out_specs=out_specs,
        ),
        out_shape=out_shape,
        compiler_params=pltpu.CompilerParams(vmem_limit_bytes=8 * 2**20),
        cost_estimate=pl.CostEstimate(
            flops=2 * 1024 * depth * width, bytes_accessed=8 * 2**20, transcendentals=0),
    )(blocks, rows, cols)


def last_kernel(pair, scaled, update, rms):
    sums = jnp.sum(pair[...], axis=0, keepdims=True)
    row_mean = jnp.sum(sums[:, 128:], axis=1, keepdims=True) / D
    total_sq = jnp.sum(sums[:, :128], axis=1, keepdims=True) * row_mean
    update_rms = jnp.sqrt(total_sq / (D * FF))
    update[...] = scaled[...] * (jnp.sqrt(row_mean) / jnp.maximum(1.0, update_rms / CLIP))
    rms[...] = jnp.broadcast_to(update_rms, rms.shape)


def last_product(pair, scaled):
    rows, cols = scaled.shape
    return pl.pallas_call(
        last_kernel,
        grid=(2,),
        in_specs=[
            pl.BlockSpec(pair.shape, lambda i: (0, 0)),
            pl.BlockSpec((rows // 2, cols), lambda i: (i, 0)),
        ],
        out_specs=[
            pl.BlockSpec((rows // 2, cols), lambda i: (i, 0)),
            pl.BlockSpec((8, 128), lambda i: (0, 0)),
        ],
        out_shape=[
            jax.ShapeDtypeStruct(scaled.shape, jnp.float32),
            jax.ShapeDtypeStruct((8, 128), jnp.float32),
        ],
        compiler_params=pltpu.CompilerParams(vmem_limit_bytes=8 * 2**20),
    )(pair, scaled)


class Order:
    def __init__(self):
        self.last = None

    def __call__(self, value):
        if self.last is not None:
            value = after(value, self.last)
        self.last = value
        return value


class Chain:
    def __init__(self, order, axis, part):
        self.order, self.axis, self.part = order, axis, part

    def start(self):
        self.moved = swap(self.order(self.part(0)), self.axis, 0)

    def turn(self):
        got = self.order(self.moved)
        half = got.shape[0] // 2
        self.kept = got[:half]
        self.moved = swap(self.order(got[half:] + self.part(1)), self.axis, 1)

    def done(self):
        self.value = (self.order(self.moved) + self.kept) + self.part(2)


def summed_product(activations, cotangent):
    core = lax.axis_index("c")
    order = Order()

    def owners(axis):
        mine = lax.axis_index(axis)
        near, far = mine ^ 1, mine ^ 3
        return jnp.stack([
            jnp.where(core == 0, near, far), mine ^ 2, jnp.where(core == 0, far, near), mine,
        ]).astype(jnp.int32)

    def columns(chunk):
        return cotangent[:, slice(*COLS[chunk])]

    def quarters(rows):
        size = rows.shape[0] // 4
        return (rows[:2 * size], rows[2 * size:3 * size], rows[3 * size:])

    def product_chain(axis, chunk, first=None):
        def part(i):
            if i == 0 and first is not None:
                return first
            return jnp.dot(lhs[axis][i], columns(chunk), preferred_element_type=jnp.float32)

        return Chain(order, axis, part)

    def next_chain(chain):
        parts = quarters(chain.value)
        return Chain(order, "zh" if chain.axis == "y" else "y", lambda i: parts[i])

    blocks = (owners("y")[:, None] + 4 * owners("zh")[None, :]).reshape(16)
    first, = early_product(first_kernel, blocks[:8], activations, columns("a"))
    a = product_chain("y", "a", first)
    a.start()
    first, by_y, by_zh = early_product(
        second_kernel, order(blocks), activations, columns("b"))
    lhs = {"y": quarters(by_y), "zh": quarters(by_zh)}
    b = product_chain("y", "b", first)
    b.start()
    c, d, f = (product_chain("y", chunk) for chunk in "cdf")
    e = product_chain("zh", "e")
    e.start()
    a.turn()
    a.done()
    c.start()
    a = next_chain(a)
    a.start()
    b.turn()
    e.turn()
    a.turn()
    b.done()
    c.turn()
    b = next_chain(b)
    b.start()
    a.done()
    e.done()
    e = next_chain(e)
    e.start()
    d.start()
    b.turn()
    c.done()
    c = next_chain(c)
    c.start()
    f.start()
    d.turn()
    e.turn()
    f.turn()
    b.done()
    c.turn()
    d.done()
    d = next_chain(d)
    d.start()
    f.done()
    f = next_chain(f)
    f.start()
    d.turn()
    f.turn()
    e.done()
    c.done()
    d.done()
    f.done()
    return [chain.value for chain in (a, b, c, d, f, e)]


def per_device(activations, cotangent, row_old, col_old):
    grads = summed_product(activations, cotangent)
    squares = [g * g + EPS_ONE for g in grads]
    col_total = jnp.concatenate([jnp.sum(s, axis=0) for s in squares])
    row_total = sum(jnp.sum(s, axis=1) for s in squares)
    col_total = spread_sum(col_total, ("zh", "y", "zl"), 32)
    col_new = DECAY * col_old + (1.0 - DECAY) * (col_total / D)
    grad = jnp.concatenate(grads, axis=1)
    rows = jnp.stack([row_total, jnp.sum(grad * grad / col_new[None, :], axis=1)])
    rows = rows + lax.ppermute(rows, "c", [(0, 1), (1, 0)])
    rows = rows + sum(
        lax.ppermute(rows, "x", [(i, (i + d) % 4) for i in range(4)]) for d in (1, 2, 3))
    row_new = DECAY * row_old + (1.0 - DECAY) * (rows[0] / FF)
    pair = jnp.concatenate([rows[1] / row_new, row_new])
    pair = jnp.broadcast_to(pair[None], (32, 256))
    pair = lax.all_to_all(pair, ("zh", "y", "zl"), 0, 0)
    scaled = grad * lax.rsqrt(row_new)[:, None] * lax.rsqrt(col_new)[None, :]
    update, update_rms = last_product(pair, scaled)
    return (update, row_new, col_new, update_rms[0, 0])


def solution(mesh):
    mesh = Mesh(mesh.devices.reshape(4, 4, 2, 4, 2), AXES)
    dp, col = ("zh", "y"), ("x", "c")
    in_specs = (P(dp, "zl"), P(dp, col), P(("zl",) + dp), P(col))
    out_specs = (P(("zl",) + dp, col), P(("zl",) + dp), P(col), P())
    return jax.shard_map(
        per_device, mesh=mesh, in_specs=in_specs, out_specs=out_specs, check_vma=False
    )
```
